128 devices in a mesh: dp: 4 (over y_hi, core), expert: 32 (over y_lo, x, z).
Axes of the slice: x: 4, y: 4 (y_hi: 2, y_lo: 2; y = y_hi * 2 + y_lo), z: 4, core: 2. Of those that a mesh axis runs over, the one named last changes fastest.
Arguments:
- tokens: bfloat16 [16384, 2048], P(('dp', 'expert')), may hold values from -6 to 6
- d_mixed: bfloat16 [16384, 2048], P(('dp', 'expert')), may hold values from -6 to 6
- w_in: bfloat16 [128, 2048, 768], P('expert'), may hold values from -0.125 to 0.125
- w_out: bfloat16 [128, 384, 2048], P('expert'), may hold values from -0.3125 to 0.3125
- expert_ids: int32 [16384, 8], P(('dp', 'expert')), may hold values from 0 to 127, all different within a row; in each aligned block of 128 rows (0 to 127, 128 to 255, ...) at most 10 rows name the same one
- gate_fixed: int32 [16384, 8], P(('dp', 'expert')), may hold values from 1 to 65535
- placement: int32 [128], replicated, may hold values from 0 to 127, each once
Outputs:
- mixed: bfloat16 [16384, 2048], P(('dp', 'expert'))
- d_tokens: bfloat16 [16384, 2048], P(('dp', 'expert'))
- grad_in: bfloat16 [128, 2048, 768], P('expert', 'dp')
- grad_out: bfloat16 [128, 384, 2048], P('expert', None, 'dp')
The draws below stay inside these ranges and needn't reach their ends.
Inputs may be any that keep to these rules, and one draw needn't show every extreme that they name: `expert_ids`: each row names 8 different experts. Among the rows of one device no expert is named more than 10 times, and in every draw some expert is named exactly 10 times by the rows of some device. Each number appears once: expert e's weights are in slot placement[e], held by expert-axis index placement[e] // 4.
All inputs are finite; a program needn't handle non-finite values.
Results may differ from the reference program's by a relative error of at most 0.009.
Values may be sent and summed in bfloat16 or wider, within the bound.
A program may use at most 192 MiB of HBM per device.

```python
import math
import jax
import jax.numpy as jnp
import numpy as np
from jax import lax

D = 2048
FF = 384
TOP = 8
TOK_DEV = 128
EXPERTS = 128
TOKENS = 16384
CAP = 10
N_DP = 4
N_EXPERT = 32


def touch_ends(drawn, key, least, high):
    extent = drawn.shape
    place = [jax.random.randint(jax.random.fold_in(key, axis), (), 0, extent[axis]) for axis in range(len(extent))]
    drawn = drawn.at[tuple(place)].set(least)
    longest = extent.index(max(extent))
    place[longest] = (place[longest] + 1) % extent[longest]
    return drawn.at[tuple(place)].set(high)


def shard_levels(own_key, shape, shards, low, high):
    loudness, own = 1.0, jax.random.fold_in(own_key, 6)
    for dim, shards_of in shards:
        heights = jnp.exp(jax.random.uniform(jax.random.fold_in(own, dim), (shards_of,), jnp.float32, low / len(shards), high / len(shards)))
        loudness = loudness * jnp.repeat(heights, shape[dim] // shards_of).reshape([-1 if axis == dim else 1 for axis in range(len(shape))])
    return loudness


def shared_out(rng, own, number, rows, count, top, bound, skew):
    sequence = jax.random.permutation(rng, count)
    heavy_load, usual = portions_of(count, rows * top, bound, skew, True), portions_of(count, rows * top, bound, skew, False)
    places = jnp.arange(count)

    def named(sizes, turn):
        used = int((sizes > 0).sum())
        fixed = max(1, used // 4)
        passed = fixed + (places - fixed + turn * (used - fixed)) % max(1, count - fixed)
        return jnp.zeros((count,), jnp.int32).at[sequence[jnp.where(places < fixed, places, passed)]].set(jnp.asarray(sizes, jnp.int32))

    sizes = jnp.where(number % 4 == 0, named(heavy_load, number // 4), named(usual, number - number // 4 - 1))
    mixed = jax.random.permutation(jax.random.fold_in(own, 3), count)
    donor, receiver = mixed[0:count // 2 * 2:2], mixed[1:count // 2 * 2:2]
    margin = jnp.minimum(sizes[donor] - 1, bound - sizes[receiver]) // 2
    margin = jnp.where((donor == sequence[0]) | (receiver == sequence[0]) | (sizes[receiver] == 0), 0, jnp.maximum(margin, 0))
    passed = jax.random.randint(jax.random.fold_in(own, 4), (count // 2,), 0, 1 << 20) % (margin + 1)
    sizes = sizes.at[donor].add(-passed).at[receiver].add(passed)
    items = jnp.searchsorted(jnp.cumsum(sizes), jnp.arange(rows * top), side="right").astype(jnp.int32)
    grid = items.reshape(top, rows).T
    grid = grid[jax.random.permutation(jax.random.fold_in(own, 1), rows)]
    turn = jax.random.randint(jax.random.fold_in(own, 2), (rows, 1), 0, top)
    return jnp.take_along_axis(grid, (jnp.arange(top)[None, :] + turn) % top, axis=1)


def portions_of(amount, total, most, skew, full):
    weights = [(1 << 20) // math.isqrt(rank ** skew) + 1 for rank in range(1, amount + 1)]
    largest = most if full else min(most, max(-(-total // amount), total * weights[0] // sum(weights)))
    least = 1 if total - largest >= amount - 1 else 0
    holding, rest = [largest] + [least] * (amount - 1), total - largest - least * (amount - 1)
    while rest > 0:
        candidates = [i for i in range(1, amount) if holding[i] < largest] or [i for i in range(1, amount) if holding[i] < most]
        mass, budget = sum([weights[i] for i in candidates]), rest
        for i in candidates:
            addition = min(most - holding[i], max(1, budget * weights[i] // mass), rest)
            holding[i] = holding[i] + addition
            rest = rest - addition
    return np.array(holding)


def centred(own_key, extent, deviation, limit, shards=(), kind=jnp.bfloat16):
    drawn = jax.random.normal(own_key, extent, jnp.float32) * deviation
    if len(shards) > 0:
        drawn = shard_levels(own_key, extent, shards, -0.22, 0.18) * drawn
    return jnp.clip(drawn, min=-limit, max=limit).astype(kind)


def setup_inputs(seed: int = 0) -> dict:
    keys = jax.random.split(jax.random.key(seed), 8)
    tokens = centred(keys[0], (TOKENS, D), 1.0, 6.0, ((0, 128),))
    d_mixed = centred(keys[1], (TOKENS, D), 1.0, 6.0, ((0, 128),))
    w_in = centred(keys[2], (EXPERTS, D, 2 * FF), D ** -0.5, 0.125, ((0, 32),))
    w_out = centred(keys[3], (EXPERTS, FF, D), FF ** -0.5, 0.3125, ((0, 32),))
    expert_ids_keys = jax.random.split(jax.random.fold_in(keys[4], 1), TOKENS // TOK_DEV)
    expert_ids_turns = jax.random.permutation(jax.random.fold_in(keys[4], 3), TOKENS // TOK_DEV)
    expert_ids = jax.vmap(lambda own, number: shared_out(jax.random.fold_in(keys[4], 2), own, number, TOK_DEV, EXPERTS, TOP, CAP, 2))(expert_ids_keys, expert_ids_turns).reshape((TOKENS, TOP))
    gate_fixed = touch_ends(jax.random.randint(keys[5], (TOKENS, TOP), 1, 65536), jax.random.fold_in(keys[5], 1), 1, 65535).astype(jnp.int32)
    placement = jax.random.permutation(keys[6], EXPERTS).astype(jnp.int32)
    return {"tokens": tokens, "d_mixed": d_mixed, "w_in": w_in, "w_out": w_out, "expert_ids": expert_ids, "gate_fixed": gate_fixed, "placement": placement}


def reference(tokens, d_mixed, w_in, w_out, expert_ids, gate_fixed, placement):
    blocks = N_DP * N_EXPERT
    rows_slot = blocks * CAP
    gates = gate_fixed.astype(jnp.float32)
    gates = gates / jnp.sum(gates, axis=1, keepdims=True)
    slot = placement[expert_ids].astype(jnp.int32)
    block_slot = slot.reshape(blocks, TOK_DEV * TOP)
    catalog = jnp.arange(EXPERTS, dtype=jnp.int32)
    onehot = (block_slot[:, :, None] == catalog).astype(jnp.int32)
    rank = jnp.sum(jnp.cumsum(onehot, axis=1) * onehot, axis=2) - 1
    block_index = jnp.arange(blocks, dtype=jnp.int32)[:, None]
    dest = (block_slot * rows_slot + block_index * CAP + rank).astype(jnp.int32)
    dest = dest.reshape(TOKENS, TOP)
    token_index = jnp.broadcast_to(jnp.arange(TOKENS, dtype=jnp.int32)[:, None], (TOKENS, TOP))
    source = jnp.full((EXPERTS * rows_slot,), TOKENS, dtype=jnp.int32)
    source = source.at[dest.reshape(-1)].set(token_index.reshape(-1)).reshape(EXPERTS, rows_slot)
    slot_gate = jnp.zeros((EXPERTS * rows_slot,), jnp.float32)
    slot_gate = slot_gate.at[dest.reshape(-1)].set(gates.reshape(-1)).reshape(EXPERTS, rows_slot)
    zero_row = jnp.zeros((1, D), jnp.bfloat16)
    x_padded = jnp.concatenate([tokens, zero_row], axis=0)
    d_padded = jnp.concatenate([d_mixed, zero_row], axis=0)

    def one_slot(items):
        picks, slot_g, wi, wo = items
        rows = x_padded[picks]
        pre = jnp.dot(rows, wi, preferred_element_type=jnp.float32)
        gate = pre[:, :FF]
        up = pre[:, FF:]
        sig = jax.nn.sigmoid(gate)
        silu = gate * sig
        act = (silu * up).astype(jnp.bfloat16)
        out = jnp.dot(act, wo, preferred_element_type=jnp.float32).astype(jnp.bfloat16)
        d_exp = (slot_g[:, None] * d_padded[picks].astype(jnp.float32)).astype(jnp.bfloat16)
        d_act = jnp.dot(d_exp, wo.T, preferred_element_type=jnp.float32)
        d_gate = d_act * up * sig * (1.0 + gate * (1.0 - sig))
        d_up = d_act * silu
        d_pre = jnp.concatenate([d_gate, d_up], axis=1).astype(jnp.bfloat16)
        d_rows = jnp.dot(d_pre, wi.T, preferred_element_type=jnp.float32).astype(jnp.bfloat16)
        act_g = act.reshape(N_DP, -1, FF).astype(jnp.float32)
        dexp_g = d_exp.reshape(N_DP, -1, D).astype(jnp.float32)
        rows_g = rows.reshape(N_DP, -1, D).astype(jnp.float32)
        dpre_g = d_pre.reshape(N_DP, -1, 2 * FF).astype(jnp.float32)
        part_out = jnp.einsum('prf,prd->pfd', act_g, dexp_g).astype(jnp.bfloat16)
        part_in = jnp.einsum('prd,prf->pdf', rows_g, dpre_g).astype(jnp.bfloat16)
        part_out = lax.optimization_barrier(part_out)
        part_in = lax.optimization_barrier(part_in)
        g_out = jnp.sum(part_out.astype(jnp.float32), axis=0).astype(jnp.bfloat16)
        g_in = jnp.sum(part_in.astype(jnp.float32), axis=0).astype(jnp.bfloat16)
        return out, d_rows, g_in, g_out

    outs, d_all, grad_in, grad_out = lax.map(one_slot, (source, slot_gate, w_in, w_out))
    out_flat = outs.reshape(-1, D)
    d_flat = d_all.reshape(-1, D)
    mixed = jnp.zeros((TOKENS, D), jnp.float32)
    d_tokens = jnp.zeros((TOKENS, D), jnp.float32)
    for k in range(TOP):
        mixed = mixed + gates[:, k:k + 1] * out_flat[dest[:, k]].astype(jnp.float32)
        d_tokens = d_tokens + d_flat[dest[:, k]].astype(jnp.float32)
    return mixed.astype(jnp.bfloat16), d_tokens.astype(jnp.bfloat16), grad_in, grad_out
```

```python
import jax
import jax.numpy as jnp
from jax import lax
from jax.sharding import PartitionSpec as P

CAP = 10
F32 = jnp.float32
BF16 = jnp.bfloat16
ALL = ("dp", "expert")


def body(tokens, d_mixed, w_in, w_out, expert_ids, gate_fixed, placement):
    tok_rows, width = tokens.shape
    copies = lax.axis_size("dp")
    holders = lax.axis_size("expert")
    hidden = w_out.shape[1]
    devices = copies * holders
    main, rest = 8, CAP - 8
    gates = gate_fixed.astype(F32)
    gates = gates / jnp.sum(gates, axis=1, keepdims=True)
    catalog = jnp.arange(devices, dtype=jnp.int32)
    home = (placement % copies) * holders + placement // copies
    target = jnp.sum(jnp.where(expert_ids[:, :, None] == catalog, home, 0), axis=2)
    hits = target[:, :, None] == catalog
    sent = jnp.any(hits, axis=1)
    weight = jnp.sum(jnp.where(hits, gates[:, :, None], 0.0), axis=1)
    t_ids = jnp.arange(tok_rows, dtype=jnp.int32)
    before = (t_ids[:, None] > t_ids[None, :]).astype(BF16)
    rank = jnp.dot(before, sent.astype(BF16), preferred_element_type=F32).astype(jnp.int32)
    rank = jnp.where(sent, rank, -1).T
    weight = weight.T

    def picks(first, count):
        ranks = first + jnp.arange(count, dtype=jnp.int32)
        pick = rank[:, None, :] == ranks[None, :, None]
        gate = jnp.where(pick, weight[:, None, :], 0.0)
        high = gate.astype(BF16)
        low = (gate - high.astype(F32)).astype(BF16)
        flat = (devices * count, tok_rows)
        return (
            pick.astype(BF16).reshape(flat),
            jnp.sum(gate, axis=2).reshape(-1, 1),
            high.reshape(flat),
            low.reshape(flat),
        )

    parts = [picks(0, main), picks(main, rest)]
    counts = [main, rest]

    def exchange(rows, count):
        return lax.all_to_all(
            rows.reshape(devices, count, width), ALL, split_axis=0, concat_axis=0, tiled=True
        ).reshape(devices * count, width)

    def dispatch(rows, gated):
        out = []
        for (pick, scale, _, _), count in zip(parts, counts):
            chosen = jnp.dot(pick, rows, preferred_element_type=F32)
            if gated:
                chosen = chosen * scale
            out.append(exchange(chosen.astype(BF16), count))
        return jnp.concatenate(out, axis=0)

    def send_back(rows):
        cut = devices * main
        return [exchange(rows[:cut], main), exchange(rows[cut:], rest)]

    mine = lax.axis_index("dp")
    wi = lax.dynamic_index_in_dim(w_in, mine, 0, keepdims=False)
    wo = lax.dynamic_index_in_dim(w_out, mine, 0, keepdims=False)
    x = dispatch(tokens, False)
    d = dispatch(d_mixed, True)
    pre = jnp.dot(x, wi, preferred_element_type=F32)
    gate, up = pre[:, :hidden], pre[:, hidden:]
    sig = jax.nn.sigmoid(gate)
    silu = gate * sig
    act = (silu * up).astype(BF16)
    out = jnp.dot(act, wo, preferred_element_type=F32).astype(BF16)
    back = send_back(out)
    d_act = lax.dot_general(d, wo, (((1,), (1,)), ((), ())), preferred_element_type=F32)
    d_pre = jnp.concatenate(
        [d_act * up * sig * (1.0 + gate * (1.0 - sig)), d_act * silu], axis=1
    ).astype(BF16)
    d_rows = lax.dot_general(d_pre, wi, (((1,), (1,)), ((), ())), preferred_element_type=F32)
    returned = send_back(d_rows.astype(BF16))
    over_rows = (((0,), (0,)), ((), ()))
    g_in = lax.dot_general(x, d_pre, over_rows, preferred_element_type=F32).astype(BF16)
    g_out = lax.dot_general(act, d, over_rows, preferred_element_type=F32).astype(BF16)
    share = width // copies
    grad_in = lax.all_to_all(
        g_in.reshape(copies, share, 2 * hidden), "dp", split_axis=0, concat_axis=0, tiled=True
    )
    grad_out = lax.all_to_all(
        jnp.transpose(g_out.reshape(hidden, copies, share), (1, 0, 2)),
        "dp",
        split_axis=0,
        concat_axis=0,
        tiled=True,
    )
    mixed = jnp.zeros((tok_rows, width), F32)
    d_tokens = jnp.zeros((tok_rows, width), F32)
    for (pick, _, high, low), rows, d_part in zip(parts, back, returned):
        for table in (high, low):
            mixed = mixed + lax.dot_general(table, rows, over_rows, preferred_element_type=F32)
        d_tokens = d_tokens + lax.dot_general(pick, d_part, over_rows, preferred_element_type=F32)
    return mixed.astype(BF16), d_tokens.astype(BF16), grad_in, grad_out


def solution(mesh):
    in_specs = (
        P(ALL, None),
        P(ALL, None),
        P("expert", None, None),
        P("expert", None, None),
        P(ALL, None),
        P(ALL, None),
        P(),
    )
    out_specs = (P(ALL, None), P(ALL, None), P("expert", "dp", None), P("expert", None, "dp"))
    return jax.shard_map(body, mesh=mesh, in_specs=in_specs, out_specs=out_specs, check_vma=False)
```

```python
import jax
import jax.numpy as jnp
from jax import lax
from jax.experimental import pallas as pl
from jax.experimental.pallas import tpu as pltpu
from jax.sharding import PartitionSpec as P

CAP = 10
F32 = jnp.float32
BF16 = jnp.bfloat16
ALL = ("dp", "expert")
MESH = pl.DeviceIdType.MESH
RING, PLANE, CORES = 4, 16, 2
PEERS = PLANE * CORES
CHUNKS, GROUPS, TILE = 4, 5, 8
ROWS = PEERS * TILE


def dot(a, b, dims):
    return lax.dot_general(a, b, (dims, ((), ())), preferred_element_type=F32)


def flat(block):
    return block.reshape(ROWS, block.shape[-1])


def kernel(
    tokens, d_mixed, tables, w_in, w_out,
    mixed, d_tokens, grad_in, grad_out,
    x_own, d_own, x_send, d_send, x_recv, d_recv, o_recv, r_recv, m_recv, t_recv,
    tabs, wi, wo, pick, scale, back, gated, pre, act, d_pre, g_in, g_out,
    w_sem, tab_s, tab_r, own_s, own_r, send, recv, part_s, part_r, gi_s, gi_r, go_s, go_r,
):
    dp, ex = lax.axis_index("dp"), lax.axis_index("expert")
    y = (dp // CORES) * 2 + ex // PLANE
    core, place = dp % CORES, ex % PLANE
    me = core * PLANE + place
    wide = x_send.shape[-1]
    hidden = act.shape[-1]

    def ring_id(other):
        return ((other // 2) * CORES + core, (other % 2) * PLANE + place)

    def plane_id(other):
        return ((dp // CORES) * CORES + other // PLANE, (ex // PLANE) * PLANE + other % PLANE)

    def remote(src, dst, s, r, device):
        return pltpu.make_async_remote_copy(
            src_ref=src, dst_ref=dst, send_sem=s, recv_sem=r, device_id=device, device_id_type=MESH
        )

    def await_bytes(ref, sem):
        pltpu.make_async_copy(ref, ref, sem).wait()

    get_wi = pltpu.make_async_copy(w_in.at[dp], wi, w_sem.at[0])
    get_wo = pltpu.make_async_copy(w_out.at[dp], wo, w_sem.at[1])

    for i in range(1, RING):
        other = (y + i) % RING
        remote(tables.at[other], tabs.at[y], tab_s, tab_r, ring_id(other)).start()
    pltpu.make_async_copy(tables.at[y], tabs.at[y], tab_r).start()

    def spread(n, rows, own):
        for c in range(CHUNKS):
            part = rows.at[:, pl.ds(c * wide, wide)]
            for i in range(1, RING):
                other = (y + i) % RING
                remote(part, own.at[c, y], own_s.at[n, c], own_r.at[n, c], ring_id(other)).start()
            pltpu.make_async_copy(part, own.at[c, y], own_r.at[n, c]).start()

    spread(0, tokens, x_own)
    get_wi.start()
    get_wo.start()
    spread(1, d_mixed, d_own)

    await_bytes(tabs, tab_r)
    code = jnp.concatenate([tabs[s, 0] for s in range(RING)], axis=1)
    gate = jnp.concatenate([tabs[s, 1] for s in range(RING)], axis=1)
    row = lax.broadcasted_iota(jnp.int32, (PEERS, TILE, code.shape[1]), 1).astype(F32)

    for a in range(GROUPS):
        hit = code[:, None, :] == row + F32(a * TILE)
        ones = jnp.where(hit, 1.0, 0.0).astype(F32)
        pick[a] = flat(ones).astype(BF16)
        scale[a] = flat(jnp.sum(ones * gate[:, None, :], axis=2, keepdims=True))

    def exchange(n, c, out, into):
        def one(i, carry):
            other = (me + i) % PEERS
            remote(
                out.at[c, :, other], into.at[c, :, me], send.at[n, c], recv.at[n, c], plane_id(other)
            ).start()
            return carry

        lax.fori_loop(1, PEERS, one, 0)
        pltpu.make_async_copy(out.at[c, :, me], into.at[c, :, me], recv.at[n, c]).start()

    def sent(n, c, out):
        await_bytes(out.at[c, :, pl.ds(0, PEERS - 1)], send.at[n, c])

    def put(out, c, a, rows):
        out[c, a] = rows.reshape(PEERS, TILE, rows.shape[-1]).astype(BF16)

    def choose(n, own, out, into, gated_by):
        def chunk(c, carry):
            await_bytes(own.at[c], own_r.at[n, c])
            source = own[c].reshape(-1, wide)

            def group(a, carry):
                rows = dot(pick[a], source, ((1,), (0,)))
                put(out, c, a, rows * scale[a] if gated_by else rows)
                return carry

            lax.fori_loop(0, GROUPS, group, 0)
            exchange(n, c, out, into)
            return carry

        lax.fori_loop(0, CHUNKS, chunk, 0)

    choose(0, x_own, x_send, x_recv, False)
    choose(1, d_own, d_send, d_recv, True)

    repeat = lax.broadcasted_iota(jnp.int32, (PEERS, ROWS), 1) // TILE
    repeat = jnp.where(repeat == lax.broadcasted_iota(jnp.int32, (PEERS, ROWS), 0), 1.0, 0.0)
    repeat = repeat.astype(BF16)
    codes = dot(code.astype(BF16), repeat, ((0,), (0,)))
    gates = dot(gate.astype(BF16), repeat, ((0,), (0,)))
    place_of = (lax.broadcasted_iota(jnp.int32, codes.shape, 1) % TILE).astype(F32)
    for a in range(GROUPS):
        hit = codes == place_of + F32(a * TILE)
        back[a] = jnp.where(hit, 1.0, 0.0).astype(BF16)
        gated[a] = jnp.where(hit, gates, 0.0).astype(BF16)

    get_wi.wait()
    get_wo.wait()
    for c in range(CHUNKS):
        await_bytes(x_recv.at[c], recv.at[0, c])

    def forward(a, carry):
        total = jnp.zeros((ROWS, 2 * hidden), F32)
        for c in range(CHUNKS):
            total += dot(flat(x_recv[c, a]), wi[pl.ds(c * wide, wide), :], ((1,), (0,)))
        pre[a] = total
        g, up = total[:, :hidden], total[:, hidden:]
        act[a] = (g * jax.nn.sigmoid(g) * up).astype(BF16)
        return carry

    lax.fori_loop(0, GROUPS, forward, 0)

    for c in range(CHUNKS):
        sent(0, c, x_send)

        def group(a, carry, c=c):
            put(x_send, c, a, dot(act[a], wo[:, pl.ds(c * wide, wide)], ((1,), (0,))))
            return carry

        lax.fori_loop(0, GROUPS, group, 0)
        exchange(2, c, x_send, o_recv)

    for c in range(CHUNKS):
        await_bytes(d_recv.at[c], recv.at[1, c])

    def backward(a, carry):
        d_act = jnp.zeros((ROWS, hidden), F32)
        for c in range(CHUNKS):
            d_act += dot(flat(d_recv[c, a]), wo[:, pl.ds(c * wide, wide)], ((1,), (1,)))
        both = pre[a]
        g, up = both[:, :hidden], both[:, hidden:]
        sig = jax.nn.sigmoid(g)
        d_pre[a, :, pl.ds(0, hidden)] = (d_act * up * sig * (1.0 + g * (1.0 - sig))).astype(BF16)
        d_pre[a, :, pl.ds(hidden, hidden)] = (d_act * (g * sig)).astype(BF16)
        return carry

    lax.fori_loop(0, GROUPS, backward, 0)

    for c in range(CHUNKS):
        sent(1, c, d_send)

        def group(a, carry, c=c):
            put(d_send, c, a, dot(d_pre[a], wi[pl.ds(c * wide, wide), :], ((1,), (1,))))
            return carry

        lax.fori_loop(0, GROUPS, group, 0)
        exchange(3, c, d_send, r_recv)

    copies = []
    for i in (1, 2, 3, 0):
        c = (dp + i) % CHUNKS
        slot = i % 2
        if i in (3, 0):
            for copy in copies[(i - 3) % 4]:
                copy.wait_send()

        def grad_i(a, total, c=c):
            return total + dot(flat(x_recv[c, a]), d_pre[a], ((0,), (0,)))

        def grad_o(a, total, c=c):
            return total + dot(act[a], flat(d_recv[c, a]), ((0,), (0,)))

        g_in[slot] = lax.fori_loop(0, GROUPS, grad_i, jnp.zeros(g_in.shape[1:], F32)).astype(BF16)
        g_out[slot] = lax.fori_loop(0, GROUPS, grad_o, jnp.zeros(g_out.shape[1:], F32)).astype(BF16)
        if i:
            pair = [
                remote(g_in.at[slot], grad_in.at[dp], gi_s.at[i], gi_r.at[i], (c, ex)),
                remote(g_out.at[slot], grad_out.at[dp], go_s.at[i], go_r.at[i], (c, ex)),
            ]
        else:
            pair = [
                pltpu.make_async_copy(g_in.at[slot], grad_in.at[dp], gi_s.at[i]),
                pltpu.make_async_copy(g_out.at[slot], grad_out.at[dp], go_s.at[i]),
            ]
        for copy in pair:
            copy.start()
        copies.append(pair)

    def gather(n, weights, came, own, parts):
        for c in range(CHUNKS):
            await_bytes(came.at[c], recv.at[n + 2, c])

            def group(a, total, c=c):
                return total + dot(weights[a], flat(came[c, a]), ((1,), (0,)))

            total = lax.fori_loop(0, GROUPS, group, jnp.zeros((RING * own.shape[2], wide), F32))
            await_bytes(own.at[c, pl.ds(0, RING - 1)], own_s.at[n, c])
            own[c] = total.reshape(RING, -1, wide).astype(BF16)
            for i in range(1, RING):
                other = (y + i) % RING
                remote(
                    own.at[c, other], parts.at[c, i - 1], part_s.at[n, c], part_r.at[n, c], ring_id(other)
                ).start()

    def finish(n, own, parts, out):
        for c in range(CHUNKS):
            await_bytes(parts.at[c], part_r.at[n, c])
            total = own[c, y].astype(F32)
            for i in range(RING - 1):
                total += parts[c, i].astype(F32)
            out[:, pl.ds(c * wide, wide)] = total.astype(BF16)

    gather(0, gated, o_recv, x_own, m_recv)
    gather(1, back, r_recv, d_own, t_recv)
    finish(0, x_own, m_recv, mixed)
    finish(1, d_own, t_recv, d_tokens)

    for c in range(CHUNKS):
        sent(2, c, x_send)
        sent(3, c, d_send)
        for n, own in ((0, x_own), (1, d_own)):
            await_bytes(own.at[c, pl.ds(0, RING - 1)], part_s.at[n, c])
    await_bytes(tabs.at[pl.ds(0, RING - 1)], tab_s)
    for copy in copies[2]:
        copy.wait_send()
    for copy in copies[3]:
        copy.wait()
    for pair in copies[:3]:
        for copy in pair:
            copy.wait_recv()


def body(tokens, d_mixed, w_in, w_out, expert_ids, gate_fixed, placement):
    tok_rows, width = tokens.shape
    hidden = w_out.shape[1]
    wide = width // CHUNKS
    experts = RING * PEERS
    gates = gate_fixed.astype(F32)
    gates = gates / jnp.sum(gates, axis=1, keepdims=True)
    catalog = jnp.arange(experts, dtype=jnp.int32)
    copy, holder = placement % RING, placement // RING
    home = ((copy // CORES) * 2 + holder // PLANE) * PEERS + (copy % CORES) * PLANE + holder % PLANE
    target = jnp.sum(jnp.where(expert_ids[:, :, None] == catalog, home, 0), axis=2)
    hits = target[:, :, None] == catalog
    sent = jnp.any(hits, axis=1)
    weight = jnp.sum(jnp.where(hits, gates[:, :, None], 0.0), axis=1)
    t_ids = jnp.arange(tok_rows, dtype=jnp.int32)
    before = (t_ids[:, None] > t_ids[None, :]).astype(BF16)
    rank = jnp.dot(before, sent.astype(BF16), preferred_element_type=F32)
    y = (lax.axis_index("dp") // CORES) * 2 + lax.axis_index("expert") // PLANE
    code = jnp.where(sent, rank * RING + y.astype(F32), -1.0)
    tables = jnp.stack([code.T, weight.T]).reshape(2, RING, PEERS, tok_rows).transpose(1, 0, 2, 3)

    shuttle = pltpu.VMEM((CHUNKS, GROUPS, PEERS, TILE, wide), BF16)
    own = pltpu.VMEM((CHUNKS, RING, tok_rows, wide), BF16)
    parts = pltpu.VMEM((CHUNKS, RING - 1, tok_rows, wide), BF16)
    dma = pltpu.SemaphoreType.DMA
    anywhere = pl.BlockSpec(memory_space=pl.ANY)
    inside = pl.BlockSpec(memory_space=pltpu.VMEM)
    all_tokens = RING * tok_rows
    return pl.pallas_call(
        kernel,
        out_shape=(
            jax.ShapeDtypeStruct((tok_rows, width), BF16),
            jax.ShapeDtypeStruct((tok_rows, width), BF16),
            jax.ShapeDtypeStruct((RING, wide, 2 * hidden), BF16),
            jax.ShapeDtypeStruct((RING, hidden, wide), BF16),
        ),
        in_specs=[anywhere] * 5,
        out_specs=(inside, inside, anywhere, anywhere),
        scratch_shapes=[
            own, own, shuttle, shuttle, shuttle, shuttle, shuttle, shuttle, parts, parts,
            pltpu.VMEM((RING, 2, PEERS, tok_rows), F32),
            pltpu.VMEM((width, 2 * hidden), BF16),
            pltpu.VMEM((hidden, width), BF16),
            pltpu.VMEM((GROUPS, ROWS, all_tokens), BF16),
            pltpu.VMEM((GROUPS, ROWS, 1), F32),
            pltpu.VMEM((GROUPS, all_tokens, ROWS), BF16),
            pltpu.VMEM((GROUPS, all_tokens, ROWS), BF16),
            pltpu.VMEM((GROUPS, ROWS, 2 * hidden), F32),
            pltpu.VMEM((GROUPS, ROWS, hidden), BF16),
            pltpu.VMEM((GROUPS, ROWS, 2 * hidden), BF16),
            pltpu.VMEM((2, wide, 2 * hidden), BF16),
            pltpu.VMEM((2, hidden, wide), BF16),
            dma((2,)), dma, dma, dma((2, CHUNKS)), dma((2, CHUNKS)),
            dma((4, CHUNKS)), dma((4, CHUNKS)), dma((2, CHUNKS)), dma((2, CHUNKS)),
            dma((4,)), dma((4,)), dma((4,)), dma((4,)),
        ],
        compiler_params=pltpu.CompilerParams(
            has_side_effects=True, vmem_limit_bytes=60 * 1024 * 1024
        ),
        cost_estimate=pl.CostEstimate(flops=36 * 10**9, bytes_accessed=30 * 10**6, transcendentals=10**6),
    )(tokens, d_mixed, tables, w_in, w_out)


def solution(mesh):
    in_specs = (
        P(ALL, None),
        P(ALL, None),
        P("expert", None, None),
        P("expert", None, None),
        P(ALL, None),
        P(ALL, None),
        P(),
    )
    out_specs = (P(ALL, None), P(ALL, None), P("expert", "dp", None), P("expert", None, "dp"))
    return jax.shard_map(body, mesh=mesh, in_specs=in_specs, out_specs=out_specs, check_vma=False)
```

```python
import jax
import jax.numpy as jnp
from jax import lax
from jax.experimental import pallas as pl
from jax.experimental.pallas import tpu as pltpu
from jax.sharding import PartitionSpec as P

CAP = 10
F32 = jnp.float32
BF16 = jnp.bfloat16
ALL = ("dp", "expert")
MESH = pl.DeviceIdType.MESH
RING, PLANE, CORES = 4, 16, 2
PEERS = PLANE * CORES
CHUNKS, GROUPS, TILE = 4, 5, 8
ROWS = PEERS * TILE
EXPERTS = RING * PEERS
ALONG = "yxzy"
BATCHES = ((0,), (1, 2, 3))
D_BATCHES = ((0, 1, 2, 3),)
RINGS = "yxz"


def dot(a, b, dims):
    return lax.dot_general(a, b, (dims, ((), ())), preferred_element_type=F32)


def times(a, b):
    return dot(a, b, ((1,), (0,)))


def flat(block):
    return block.reshape(ROWS, block.shape[-1])


def iota(shape, axis):
    return lax.broadcasted_iota(jnp.int32, shape, axis)


def ones_where(hit):
    return jnp.where(hit, 1.0, 0.0).astype(BF16)


def in_plane(ring, x, y, z, core):
    first, last = {"y": (x, z), "x": (y, z), "z": (x, y)}[ring]
    return core * PLANE + first * RING + last


def kernel(
    tokens, d_mixed, ids, fixed, placement, w_in, w_out,
    m_parts, t_parts, grad_in, grad_out,
    x_own, d_own, x_send, d_send, x_recv, d_recv, o_recv, r_recv,
    tables, tabs, wi, wo, pick, scale, order, back, gated, pre, act, d_pre, g_in, g_out,
    w_sem, tab_s, tab_r, own_s, own_r, send, recv, part_s, part_r, gi_s, gi_r, go_s, go_r,
):
    dp, ex = lax.axis_index("dp"), lax.axis_index("expert")
    core, y_hi, y_lo = dp % CORES, dp // CORES, ex // PLANE
    x, y, z = (ex // RING) % RING, y_hi * 2 + y_lo, ex % RING
    at = {"x": x, "y": y, "z": z}
    me = {ring: in_plane(ring, x, y, z, core) for ring in RINGS}
    wide = x_send.shape[-1]
    hidden = act.shape[-1]

    def device(x, y, z, core):
        return ((y // 2) * CORES + core, (y % 2) * PLANE + x * RING + z)

    def on_ring(ring, other):
        return device(**{**at, ring: other}, core=core)

    def remote(src, dst, s, r, device):
        return pltpu.make_async_remote_copy(
            src_ref=src, dst_ref=dst, send_sem=s, recv_sem=r, device_id=device, device_id_type=MESH
        )

    def await_bytes(ref, sem):
        pltpu.make_async_copy(ref, ref, sem).wait()

    get_wi = pltpu.make_async_copy(w_in.at[dp], wi, w_sem.at[0])
    get_wo = pltpu.make_async_copy(w_out.at[dp], wo, w_sem.at[1])

    def spread(n, rows, own):
        for c, ring in enumerate(ALONG):
            part = rows.at[:, pl.ds(c * wide, wide)]
            for i in range(1, RING):
                other = (at[ring] + i) % RING
                remote(
                    part, own.at[c, at[ring]], own_s.at[n, c], own_r.at[n, c], on_ring(ring, other)
                ).start()
            pltpu.make_async_copy(part, own.at[c, at[ring]], own_r.at[n, c]).start()

    spread(0, tokens, x_own)

    tok_rows = ids.shape[1]
    square = (EXPERTS, tok_rows)
    gates = fixed[...].astype(F32)
    gates = gates / jnp.sum(gates, axis=0, keepdims=True)
    routed = jnp.zeros(square, F32)
    weight = jnp.zeros(square, F32)
    for k in range(ids.shape[0]):
        hit = ids[pl.ds(k, 1), :] == iota(square, 0)
        routed += jnp.where(hit, 1.0, 0.0)
        weight += jnp.where(hit, gates[k : k + 1, :], 0.0)
    earlier = ones_where(iota((tok_rows, tok_rows), 0) < iota((tok_rows, tok_rows), 1))
    ranks = jnp.where(routed > 0.0, times(routed.astype(BF16), earlier) * RING + 1.0, 0.0).astype(BF16)
    high = weight.astype(BF16)
    middle = (weight - high.astype(F32)).astype(BF16)
    low = (weight - high.astype(F32) - middle.astype(F32)).astype(BF16)
    slot = placement[...]
    copy, holder = slot & 3, slot >> 2
    home = {"x": (holder >> 2) & 3, "y": (copy >> 1) * 2 + (holder >> 4), "z": holder & 3}
    for t, ring in enumerate(RINGS):
        target = home[ring] * PEERS + in_plane(ring, core=copy & 1, **home)
        move = ones_where(iota((EXPERTS, EXPERTS), 0) == target)
        code = times(move, ranks)
        code = jnp.where(code > 0.0, code - 1.0 + at[ring].astype(F32), -1.0)
        gate = times(move, high) + times(move, middle) + times(move, low)
        tables[t, :, 0] = code.reshape(RING, PEERS, tok_rows)
        tables[t, :, 1] = gate.reshape(RING, PEERS, tok_rows)
        for i in range(1, RING):
            other = (at[ring] + i) % RING
            remote(
                tables.at[t, other], tabs.at[t, at[ring]], tab_s.at[t], tab_r.at[t], on_ring(ring, other)
            ).start()
        pltpu.make_async_copy(tables.at[t, at[ring]], tabs.at[t, at[ring]], tab_r.at[t]).start()

    spread(1, d_mixed, d_own)
    get_wi.start()
    get_wo.start()

    def table(t, kind):
        return jnp.concatenate([tabs[t, s, kind] for s in range(RING)], axis=1)

    everyone = RING * tok_rows
    row = iota((PEERS, TILE, everyone), 1).astype(F32)

    def make_pick(t):
        await_bytes(tabs.at[t], tab_r.at[t])
        code = table(t, 0)
        for a in range(GROUPS):
            hit = code[:, None, :] == row + F32(a * TILE)
            pick[t, a] = flat(jnp.where(hit, 1.0, 0.0)).astype(BF16)

    def make_scale(t):
        code, gate = table(t, 0), table(t, 1)
        for a in range(GROUPS):
            hit = code[:, None, :] == row + F32(a * TILE)
            scale[t, a] = flat(jnp.sum(jnp.where(hit, gate[:, None, :], 0.0), axis=2, keepdims=True))

    def exchange(several):
        def one(i, carry):
            for n, c, ring, out, into in several:
                shift = dict(zip([r for r in "xyz" if r != ring], (i // RING, i)))
                there = {r: (at[r] + shift[r]) % RING if r in shift else at[r] for r in "xyz"}
                there["core"] = (core + i // PLANE) % CORES
                remote(
                    out.at[c, :, in_plane(ring, **there)],
                    into.at[c, :, me[ring]],
                    send.at[n, c],
                    recv.at[n, c],
                    device(**there),
                ).start()
            return carry

        lax.fori_loop(1, PEERS, one, 0)
        for n, c, ring, out, into in several:
            mine = me[ring]
            pltpu.make_async_copy(out.at[c, :, mine], into.at[c, :, mine], recv.at[n, c]).start()

    def sent(n, c, out):
        await_bytes(out.at[c, :, pl.ds(0, PEERS - 1)], send.at[n, c])

    def put(out, c, a, rows):
        out[c, a] = rows.reshape(PEERS, TILE, rows.shape[-1]).astype(BF16)

    def choose(n, c, own, out):
        t = RINGS.index(ALONG[c])
        await_bytes(own.at[c], own_r.at[n, c])

        def group(a, carry):
            rows = times(pick[t, a], own[c].reshape(-1, wide))
            put(out, c, a, rows * scale[t, a] if n else rows)
            return carry

        lax.fori_loop(0, GROUPS, group, 0)

    made = set()
    for batch in BATCHES:
        for c in batch:
            t = RINGS.index(ALONG[c])
            if t not in made:
                make_pick(t)
                made.add(t)
            choose(0, c, x_own, x_send)
        exchange([(0, c, ALONG[c], x_send, x_recv) for c in batch])
    for t in sorted(made):
        make_scale(t)
    for batch in D_BATCHES:
        for c in batch:
            choose(1, c, d_own, d_send)
        exchange([(1, c, ALONG[c], d_send, d_recv) for c in batch])

    to, source = iota((ROWS, ROWS), 0), iota((ROWS, ROWS), 1)
    parts = {"x": (to >> 5) & 3, "y": to & 3, "z": (to >> 3) & 3}
    for t, ring in enumerate(RINGS[1:]):
        at_row = in_plane(ring, core=to >> 7, **parts) * TILE + ((to >> 2) & 1) * RING + parts[ring]
        order[t] = ones_where(source == at_row)

    repeat = ones_where((iota((PEERS, ROWS), 1) >> 3) == iota((PEERS, ROWS), 0))
    codes = dot(table(0, 0).astype(BF16), repeat, ((0,), (0,)))
    shares = dot(table(0, 1).astype(BF16), repeat, ((0,), (0,)))
    within = (iota(codes.shape, 1) & (TILE - 1)).astype(F32)
    for a in range(GROUPS):
        hit = codes == within + F32(a * TILE)
        back[a] = ones_where(hit)
        gated[a] = jnp.where(hit, shares, 0.0).astype(BF16)

    def arrive(n, into):
        for c, ring in enumerate(ALONG):
            await_bytes(into.at[c], recv.at[n, c])
            if ring != "y":

                def group(a, carry, c=c, t=RINGS.index(ring) - 1):
                    put(into, c, a, times(order[t], flat(into[c, a])))
                    return carry

                lax.fori_loop(0, GROUPS, group, 0)

    get_wi.wait()
    get_wo.wait()
    arrive(0, x_recv)

    def forward(a, carry):
        total = jnp.zeros((ROWS, 2 * hidden), F32)
        for c in range(CHUNKS):
            total += dot(flat(x_recv[c, a]), wi[pl.ds(c * wide, wide), :], ((1,), (0,)))
        pre[a] = total
        g, up = total[:, :hidden], total[:, hidden:]
        act[a] = (g * jax.nn.sigmoid(g) * up).astype(BF16)
        return carry

    lax.fori_loop(0, GROUPS, forward, 0)

    for c in range(CHUNKS):
        sent(0, c, x_send)

        def group(a, carry, c=c):
            put(x_send, c, a, dot(act[a], wo[:, pl.ds(c * wide, wide)], ((1,), (0,))))
            return carry

        lax.fori_loop(0, GROUPS, group, 0)
        exchange([(2, c, "y", x_send, o_recv)])

    arrive(1, d_recv)

    def backward(a, carry):
        d_act = jnp.zeros((ROWS, hidden), F32)
        for c in range(CHUNKS):
            d_act += dot(flat(d_recv[c, a]), wo[:, pl.ds(c * wide, wide)], ((1,), (1,)))
        both = pre[a]
        g, up = both[:, :hidden], both[:, hidden:]
        sig = jax.nn.sigmoid(g)
        d_pre[a, :, pl.ds(0, hidden)] = (d_act * up * sig * (1.0 + g * (1.0 - sig))).astype(BF16)
        d_pre[a, :, pl.ds(hidden, hidden)] = (d_act * (g * sig)).astype(BF16)
        return carry

    lax.fori_loop(0, GROUPS, backward, 0)

    for c in range(CHUNKS):
        sent(1, c, d_send)

        def group(a, carry, c=c):
            put(d_send, c, a, dot(d_pre[a], wi[pl.ds(c * wide, wide), :], ((1,), (1,))))
            return carry

        lax.fori_loop(0, GROUPS, group, 0)
        exchange([(3, c, "y", d_send, r_recv)])

    copies = []
    for i in (1, 2, 3, 0):
        c = (dp + i) % CHUNKS
        slot = i % 2
        if i in (3, 0):
            for copy in copies[(i - 3) % 4]:
                copy.wait_send()

        def grad_i(a, total, c=c):
            return total + dot(flat(x_recv[c, a]), d_pre[a], ((0,), (0,)))

        def grad_o(a, total, c=c):
            return total + dot(act[a], flat(d_recv[c, a]), ((0,), (0,)))

        g_in[slot] = lax.fori_loop(0, GROUPS, grad_i, jnp.zeros(g_in.shape[1:], F32)).astype(BF16)
        g_out[slot] = lax.fori_loop(0, GROUPS, grad_o, jnp.zeros(g_out.shape[1:], F32)).astype(BF16)
        if i:
            pair = [
                remote(g_in.at[slot], grad_in.at[dp], gi_s.at[i], gi_r.at[i], (c, ex)),
                remote(g_out.at[slot], grad_out.at[dp], go_s.at[i], go_r.at[i], (c, ex)),
            ]
        else:
            pair = [
                pltpu.make_async_copy(g_in.at[slot], grad_in.at[dp], gi_s.at[i]),
                pltpu.make_async_copy(g_out.at[slot], grad_out.at[dp], go_s.at[i]),
            ]
        for copy in pair:
            copy.start()
        copies.append(pair)

    def gather(n, weights, came, own, parts):
        for c in range(CHUNKS):
            await_bytes(came.at[c], recv.at[n + 2, c])

            def group(a, total, c=c):
                return total + times(weights[a], flat(came[c, a]))

            total = lax.fori_loop(0, GROUPS, group, jnp.zeros((everyone, wide), F32))
            await_bytes(own.at[c, pl.ds(0, RING - 1)], own_s.at[n, c])
            own[c] = total.reshape(RING, -1, wide).astype(BF16)
            for i in range(1, RING):
                other = (y + i) % RING
                remote(
                    own.at[c, other], parts.at[c, y], part_s.at[n, c], part_r.at[n, c], on_ring("y", other)
                ).start()
            pltpu.make_async_copy(own.at[c, y], parts.at[c, y], part_r.at[n, c]).start()

    gather(0, gated, o_recv, x_own, m_parts)
    gather(1, back, r_recv, d_own, t_parts)
    for c in range(CHUNKS):
        sent(2, c, x_send)
        sent(3, c, d_send)
        for n, own in ((0, x_own), (1, d_own)):
            await_bytes(own.at[c, pl.ds(0, RING - 1)], part_s.at[n, c])
    for t in range(len(RINGS)):
        await_bytes(tabs.at[t, pl.ds(0, RING - 1)], tab_s.at[t])
    for copy in copies[2]:
        copy.wait_send()
    for copy in copies[3]:
        copy.wait()
    for pair in copies[:3]:
        for copy in pair:
            copy.wait_recv()
    for c in range(CHUNKS):
        await_bytes(m_parts.at[c], part_r.at[0, c])
        await_bytes(t_parts.at[c], part_r.at[1, c])


def finish(
    m_parts, t_parts, from_in, from_out, mixed, d_tokens, grad_in, grad_out,
    m_held, t_held, in_held, out_held, got, grad_got, gone,
):
    gets = [
        [
            pltpu.make_async_copy(parts.at[c], into.at[c], got.at[n, c])
            for n, (parts, into) in enumerate(((m_parts, m_held), (t_parts, t_held)))
        ]
        for c in range(CHUNKS)
    ]
    through = [
        (
            pltpu.make_async_copy(source.at[e], held.at[e], grad_got.at[n, e]),
            pltpu.make_async_copy(held.at[e], to.at[e], gone.at[n, e]),
        )
        for e in range(RING)
        for n, (source, held, to) in enumerate(
            ((from_in, in_held, grad_in), (from_out, out_held, grad_out))
        )
    ]
    for get, _ in through:
        get.start()
    for pair in gets:
        for get in pair:
            get.start()
    for get, leave in through:
        get.wait()
        leave.start()
    wide = m_parts.shape[-1]
    for c in range(CHUNKS):
        for get, parts, out in zip(gets[c], (m_held, t_held), (mixed, d_tokens)):
            get.wait()
            total = parts[c, 0].astype(F32)
            for s in range(1, RING):
                total += parts[c, s].astype(F32)
            out[:, pl.ds(c * wide, wide)] = total.astype(BF16)
    for _, leave in through:
        leave.wait()


def body(tokens, d_mixed, w_in, w_out, expert_ids, gate_fixed, placement):
    tok_rows, width = tokens.shape
    hidden = w_out.shape[1]
    wide = width // CHUNKS
    shuttle = pltpu.VMEM((CHUNKS, GROUPS, PEERS, TILE, wide), BF16)
    own = pltpu.VMEM((CHUNKS, RING, tok_rows, wide), BF16)
    dma = pltpu.SemaphoreType.DMA
    anywhere = pl.BlockSpec(memory_space=pl.ANY)
    inside = pl.BlockSpec(memory_space=pltpu.VMEM)
    everyone = RING * tok_rows
    kinds = len(RINGS)
    whole = jax.ShapeDtypeStruct((tok_rows, width), BF16)
    part = jax.ShapeDtypeStruct((CHUNKS, RING, tok_rows, wide), BF16)
    grads = (
        jax.ShapeDtypeStruct((RING, wide, 2 * hidden), BF16),
        jax.ShapeDtypeStruct((RING, hidden, wide), BF16),
    )
    found = pl.pallas_call(
        kernel,
        out_shape=(part, part, *grads),
        in_specs=[anywhere, anywhere, inside, inside, inside, anywhere, anywhere],
        out_specs=[anywhere] * 4,
        scratch_shapes=[
            own, own, shuttle, shuttle, shuttle, shuttle, shuttle, shuttle,
            pltpu.VMEM((kinds, RING, 2, PEERS, tok_rows), F32),
            pltpu.VMEM((kinds, RING, 2, PEERS, tok_rows), F32),
            pltpu.VMEM((width, 2 * hidden), BF16),
            pltpu.VMEM((hidden, width), BF16),
            pltpu.VMEM((kinds, GROUPS, ROWS, everyone), BF16),
            pltpu.VMEM((kinds, GROUPS, ROWS, 1), F32),
            pltpu.VMEM((max(kinds - 1, 1), ROWS, ROWS), BF16),
            pltpu.VMEM((GROUPS, everyone, ROWS), BF16),
            pltpu.VMEM((GROUPS, everyone, ROWS), BF16),
            pltpu.VMEM((GROUPS, ROWS, 2 * hidden), F32),
            pltpu.VMEM((GROUPS, ROWS, hidden), BF16),
            pltpu.VMEM((GROUPS, ROWS, 2 * hidden), BF16),
            pltpu.VMEM((2, wide, 2 * hidden), BF16),
            pltpu.VMEM((2, hidden, wide), BF16),
            dma((2,)), dma((kinds,)), dma((kinds,)), dma((2, CHUNKS)), dma((2, CHUNKS)),
            dma((4, CHUNKS)), dma((4, CHUNKS)), dma((2, CHUNKS)), dma((2, CHUNKS)),
            dma((4,)), dma((4,)), dma((4,)), dma((4,)),
        ],
        compiler_params=pltpu.CompilerParams(
            has_side_effects=True, vmem_limit_bytes=60 * 1024 * 1024
        ),
        cost_estimate=pl.CostEstimate(flops=36 * 10**9, bytes_accessed=30 * 10**6, transcendentals=10**6),
    )(tokens, d_mixed, expert_ids.T, gate_fixed.T, placement.reshape(1, -1), w_in, w_out)
    return pl.pallas_call(
        finish,
        out_shape=(whole, whole, *grads),
        in_specs=[anywhere] * 4,
        out_specs=(inside, inside, anywhere, anywhere),
        scratch_shapes=[
            *[pltpu.VMEM(held.shape, BF16) for held in (part, part, *grads)],
            dma((2, CHUNKS)), dma((2, RING)), dma((2, RING)),
        ],
        compiler_params=pltpu.CompilerParams(vmem_limit_bytes=60 * 1024 * 1024),
    )(*found)


def solution(mesh):
    in_specs = (
        P(ALL, None),
        P(ALL, None),
        P("expert", None, None),
        P("expert", None, None),
        P(ALL, None),
        P(ALL, None),
        P(),
    )
    out_specs = (P(ALL, None), P(ALL, None), P("expert", "dp", None), P("expert", None, "dp"))
    return jax.shard_map(body, mesh=mesh, in_specs=in_specs, out_specs=out_specs, check_vma=False)
```

```python
import jax
import jax.numpy as jnp
from jax import lax
from jax.experimental import pallas as pl
from jax.experimental.pallas import tpu as pltpu
from jax.sharding import PartitionSpec as P

CAP = 10
F32 = jnp.float32
BF16 = jnp.bfloat16
ALL = ("dp", "expert")
MESH = pl.DeviceIdType.MESH
RING, PLANE, CORES = 4, 16, 2
PEERS = PLANE * CORES
CHUNKS, GROUPS, TILE = 4, 5, 8
ROWS = PEERS * TILE
EXPERTS = RING * PEERS
ALONG = "yxzy"
BATCHES = ((0,), (1, 2, 3))
D_BATCHES = ((0, 1, 2, 3),)
RINGS = "yxz"


def dot(a, b, dims):
    return lax.dot_general(a, b, (dims, ((), ())), preferred_element_type=F32)


def times(a, b):
    return dot(a, b, ((1,), (0,)))


def flat(block):
    return block.reshape(ROWS, block.shape[-1])


def iota(shape, axis):
    return lax.broadcasted_iota(jnp.int32, shape, axis)


def ones_where(hit):
    return jnp.where(hit, 1.0, 0.0).astype(BF16)


def in_plane(ring, x, y, z, core):
    first, last = {"y": (x, z), "x": (y, z), "z": (x, y)}[ring]
    return core * PLANE + first * RING + last


def kernel(
    tokens, d_mixed, ids, fixed, placement, w_in, w_out,
    m_parts, t_parts, grad_in, grad_out,
    x_own, d_own, x_send, d_send, x_recv, d_recv, o_recv, r_recv,
    tables, tabs, wi, wo, pick, scale, order, back, gated, pre, act, d_pre, g_in, g_out,
    w_sem, tab_s, tab_r, own_s, own_r, send, recv, part_s, part_r, gi_s, gi_r, go_s, go_r,
):
    dp, ex = lax.axis_index("dp"), lax.axis_index("expert")
    core, y_hi, y_lo = dp % CORES, dp // CORES, ex // PLANE
    x, y, z = (ex // RING) % RING, y_hi * 2 + y_lo, ex % RING
    at = {"x": x, "y": y, "z": z}
    me = {ring: in_plane(ring, x, y, z, core) for ring in RINGS}
    wide = x_send.shape[-1]
    hidden = act.shape[-1]

    def device(x, y, z, core):
        return ((y // 2) * CORES + core, (y % 2) * PLANE + x * RING + z)

    def on_ring(ring, other):
        return device(**{**at, ring: other}, core=core)

    def remote(src, dst, s, r, device):
        return pltpu.make_async_remote_copy(
            src_ref=src, dst_ref=dst, send_sem=s, recv_sem=r, device_id=device, device_id_type=MESH
        )

    def await_bytes(ref, sem):
        pltpu.make_async_copy(ref, ref, sem).wait()

    get_wi = pltpu.make_async_copy(w_in.at[dp], wi, w_sem.at[0])
    get_wo = pltpu.make_async_copy(w_out.at[dp], wo, w_sem.at[1])

    def spread(n, rows, own, chunks):
        for c in chunks:
            ring = ALONG[c]
            part = rows.at[:, pl.ds(c * wide, wide)]
            for i in range(1, RING):
                other = (at[ring] + i) % RING
                remote(
                    part, own.at[c, at[ring]], own_s.at[n, c], own_r.at[n, c], on_ring(ring, other)
                ).start()
            pltpu.make_async_copy(part, own.at[c, at[ring]], own_r.at[n, c]).start()

    spread(0, tokens, x_own, range(1))

    tok_rows = ids.shape[1]
    square = (EXPERTS, tok_rows)
    gates = fixed[...].astype(F32)
    gates = gates / jnp.sum(gates, axis=0, keepdims=True)
    routed = jnp.zeros(square, F32)
    weight = jnp.zeros(square, F32)
    for k in range(ids.shape[0]):
        hit = ids[pl.ds(k, 1), :] == iota(square, 0)
        routed += jnp.where(hit, 1.0, 0.0)
        weight += jnp.where(hit, gates[k : k + 1, :], 0.0)
    earlier = ones_where(iota((tok_rows, tok_rows), 0) < iota((tok_rows, tok_rows), 1))
    ranks = jnp.where(routed > 0.0, times(routed.astype(BF16), earlier) * RING + 1.0, 0.0).astype(BF16)
    high = weight.astype(BF16)
    middle = (weight - high.astype(F32)).astype(BF16)
    low = (weight - high.astype(F32) - middle.astype(F32)).astype(BF16)
    slot = placement[...]
    copy, holder = slot & 3, slot >> 2
    home = {"x": (holder >> 2) & 3, "y": (copy >> 1) * 2 + (holder >> 4), "z": holder & 3}
    for t, ring in enumerate(RINGS):
        target = home[ring] * PEERS + in_plane(ring, core=copy & 1, **home)
        move = ones_where(iota((EXPERTS, EXPERTS), 0) == target)
        code = times(move, ranks)
        code = jnp.where(code > 0.0, code - 1.0 + at[ring].astype(F32), -1.0)
        gate = times(move, high) + times(move, middle) + times(move, low)
        tables[t, :, 0] = code.reshape(RING, PEERS, tok_rows)
        tables[t, :, 1] = gate.reshape(RING, PEERS, tok_rows)
        for i in range(1, RING):
            other = (at[ring] + i) % RING
            remote(
                tables.at[t, other], tabs.at[t, at[ring]], tab_s.at[t], tab_r.at[t], on_ring(ring, other)
            ).start()
        pltpu.make_async_copy(tables.at[t, at[ring]], tabs.at[t, at[ring]], tab_r.at[t]).start()

    spread(0, tokens, x_own, range(1, CHUNKS))
    get_wi.start()
    get_wo.start()

    def table(t, kind):
        return jnp.concatenate([tabs[t, s, kind] for s in range(RING)], axis=1)

    everyone = RING * tok_rows
    row = iota((PEERS, TILE, everyone), 1).astype(F32)

    def make_pick(t):
        await_bytes(tabs.at[t], tab_r.at[t])
        code = table(t, 0)
        for a in range(GROUPS):
            hit = code[:, None, :] == row + F32(a * TILE)
            pick[t, a] = flat(jnp.where(hit, 1.0, 0.0)).astype(BF16)

    def make_scale(t):
        code, gate = table(t, 0), table(t, 1)
        for a in range(GROUPS):
            hit = code[:, None, :] == row + F32(a * TILE)
            scale[t, a] = flat(jnp.sum(jnp.where(hit, gate[:, None, :], 0.0), axis=2, keepdims=True))

    def exchange(several):
        def one(i, carry):
            for n, c, ring, out, into in several:
                shift = dict(zip([r for r in "xyz" if r != ring], (i // RING, i)))
                there = {r: (at[r] + shift[r]) % RING if r in shift else at[r] for r in "xyz"}
                there["core"] = (core + i // PLANE) % CORES
                remote(
                    out.at[c, :, in_plane(ring, **there)],
                    into.at[c, :, me[ring]],
                    send.at[n, c],
                    recv.at[n, c],
                    device(**there),
                ).start()
            return carry

        lax.fori_loop(1, PEERS, one, 0)
        for n, c, ring, out, into in several:
            mine = me[ring]
            pltpu.make_async_copy(out.at[c, :, mine], into.at[c, :, mine], recv.at[n, c]).start()

    def sent(n, c, out):
        await_bytes(out.at[c, :, pl.ds(0, PEERS - 1)], send.at[n, c])

    def put(out, c, a, rows):
        out[c, a] = rows.reshape(PEERS, TILE, rows.shape[-1]).astype(BF16)

    def choose(n, c, own, out):
        t = RINGS.index(ALONG[c])
        await_bytes(own.at[c], own_r.at[n, c])

        def group(a, carry):
            rows = times(pick[t, a], own[c].reshape(-1, wide))
            put(out, c, a, rows * scale[t, a] if n else rows)
            return carry

        lax.fori_loop(0, GROUPS, group, 0)

    made = set()
    for batch in BATCHES:
        for c in batch:
            t = RINGS.index(ALONG[c])
            if t not in made:
                make_pick(t)
                made.add(t)
            choose(0, c, x_own, x_send)
        exchange([(0, c, ALONG[c], x_send, x_recv) for c in batch])
        if batch is BATCHES[0]:
            spread(1, d_mixed, d_own, range(CHUNKS))
    for t in sorted(made):
        make_scale(t)
    for batch in D_BATCHES:
        for c in batch:
            choose(1, c, d_own, d_send)
        exchange([(1, c, ALONG[c], d_send, d_recv) for c in batch])

    to, source = iota((ROWS, ROWS), 0), iota((ROWS, ROWS), 1)
    parts = {"x": (to >> 5) & 3, "y": to & 3, "z": (to >> 3) & 3}
    for t, ring in enumerate(RINGS[1:]):
        at_row = in_plane(ring, core=to >> 7, **parts) * TILE + ((to >> 2) & 1) * RING + parts[ring]
        order[t] = ones_where(source == at_row)

    repeat = ones_where((iota((PEERS, ROWS), 1) >> 3) == iota((PEERS, ROWS), 0))
    codes = dot(table(0, 0).astype(BF16), repeat, ((0,), (0,)))
    shares = dot(table(0, 1).astype(BF16), repeat, ((0,), (0,)))
    within = (iota(codes.shape, 1) & (TILE - 1)).astype(F32)
    for a in range(GROUPS):
        hit = codes == within + F32(a * TILE)
        back[a] = ones_where(hit)
        gated[a] = jnp.where(hit, shares, 0.0).astype(BF16)

    def arrive(n, into):
        for c, ring in enumerate(ALONG):
            await_bytes(into.at[c], recv.at[n, c])
            if ring != "y":

                def group(a, carry, c=c, t=RINGS.index(ring) - 1):
                    put(into, c, a, times(order[t], flat(into[c, a])))
                    return carry

                lax.fori_loop(0, GROUPS, group, 0)

    get_wi.wait()
    get_wo.wait()
    arrive(0, x_recv)

    def forward(a, carry):
        total = jnp.zeros((ROWS, 2 * hidden), F32)
        for c in range(CHUNKS):
            total += dot(flat(x_recv[c, a]), wi[pl.ds(c * wide, wide), :], ((1,), (0,)))
        pre[a] = total
        g, up = total[:, :hidden], total[:, hidden:]
        act[a] = (g * jax.nn.sigmoid(g) * up).astype(BF16)
        return carry

    lax.fori_loop(0, GROUPS, forward, 0)

    for c in range(CHUNKS):
        sent(0, c, x_send)

        def group(a, carry, c=c):
            put(x_send, c, a, dot(act[a], wo[:, pl.ds(c * wide, wide)], ((1,), (0,))))
            return carry

        lax.fori_loop(0, GROUPS, group, 0)
        exchange([(2, c, "y", x_send, o_recv)])

    arrive(1, d_recv)

    def backward(a, carry):
        d_act = jnp.zeros((ROWS, hidden), F32)
        for c in range(CHUNKS):
            d_act += dot(flat(d_recv[c, a]), wo[:, pl.ds(c * wide, wide)], ((1,), (1,)))
        both = pre[a]
        g, up = both[:, :hidden], both[:, hidden:]
        sig = jax.nn.sigmoid(g)
        d_pre[a, :, pl.ds(0, hidden)] = (d_act * up * sig * (1.0 + g * (1.0 - sig))).astype(BF16)
        d_pre[a, :, pl.ds(hidden, hidden)] = (d_act * (g * sig)).astype(BF16)
        return carry

    lax.fori_loop(0, GROUPS, backward, 0)

    for c in range(CHUNKS):
        sent(1, c, d_send)

        def group(a, carry, c=c):
            put(d_send, c, a, dot(d_pre[a], wi[pl.ds(c * wide, wide), :], ((1,), (1,))))
            return carry

        lax.fori_loop(0, GROUPS, group, 0)
        exchange([(3, c, "y", d_send, r_recv)])

    copies = []
    for i in (1, 2, 3, 0):
        c = (dp + i) % CHUNKS
        slot = i % 2
        if i in (3, 0):
            for copy in copies[(i - 3) % 4]:
                copy.wait_send()

        def grad_i(a, total, c=c):
            return total + dot(flat(x_recv[c, a]), d_pre[a], ((0,), (0,)))

        def grad_o(a, total, c=c):
            return total + dot(act[a], flat(d_recv[c, a]), ((0,), (0,)))

        g_in[slot] = lax.fori_loop(0, GROUPS, grad_i, jnp.zeros(g_in.shape[1:], F32)).astype(BF16)
        g_out[slot] = lax.fori_loop(0, GROUPS, grad_o, jnp.zeros(g_out.shape[1:], F32)).astype(BF16)
        if i:
            pair = [
                remote(g_in.at[slot], grad_in.at[dp], gi_s.at[i], gi_r.at[i], (c, ex)),
                remote(g_out.at[slot], grad_out.at[dp], go_s.at[i], go_r.at[i], (c, ex)),
            ]
        else:
            pair = [
                pltpu.make_async_copy(g_in.at[slot], grad_in.at[dp], gi_s.at[i]),
                pltpu.make_async_copy(g_out.at[slot], grad_out.at[dp], go_s.at[i]),
            ]
        for copy in pair:
            copy.start()
        copies.append(pair)

    def gather(n, weights, came, own, parts):
        for c in range(CHUNKS):
            await_bytes(came.at[c], recv.at[n + 2, c])

            def group(a, total, c=c):
                return total + times(weights[a], flat(came[c, a]))

            total = lax.fori_loop(0, GROUPS, group, jnp.zeros((everyone, wide), F32))
            await_bytes(own.at[c, pl.ds(0, RING - 1)], own_s.at[n, c])
            own[c] = total.reshape(RING, -1, wide).astype(BF16)
            for i in range(1, RING):
                other = (y + i) % RING
                remote(
                    own.at[c, other], parts.at[c, y], part_s.at[n, c], part_r.at[n, c], on_ring("y", other)
                ).start()
            pltpu.make_async_copy(own.at[c, y], parts.at[c, y], part_r.at[n, c]).start()

    gather(0, gated, o_recv, x_own, m_parts)
    gather(1, back, r_recv, d_own, t_parts)
    for c in range(CHUNKS):
        sent(2, c, x_send)
        sent(3, c, d_send)
        for n, own in ((0, x_own), (1, d_own)):
            await_bytes(own.at[c, pl.ds(0, RING - 1)], part_s.at[n, c])
    for t in range(len(RINGS)):
        await_bytes(tabs.at[t, pl.ds(0, RING - 1)], tab_s.at[t])
    for copy in copies[2]:
        copy.wait_send()
    for copy in copies[3]:
        copy.wait()
    for pair in copies[:3]:
        for copy in pair:
            copy.wait_recv()
    for c in range(CHUNKS):
        await_bytes(m_parts.at[c], part_r.at[0, c])
        await_bytes(t_parts.at[c], part_r.at[1, c])


def finish(
    m_parts, t_parts, from_in, from_out, mixed, d_tokens, grad_in, grad_out,
    m_held, t_held, in_held, out_held, got, grad_got, gone,
):
    gets = [
        [
            pltpu.make_async_copy(parts.at[c], into.at[c], got.at[n, c])
            for n, (parts, into) in enumerate(((m_parts, m_held), (t_parts, t_held)))
        ]
        for c in range(CHUNKS)
    ]
    through = [
        (
            pltpu.make_async_copy(source.at[e], held.at[e], grad_got.at[n, e]),
            pltpu.make_async_copy(held.at[e], to.at[e], gone.at[n, e]),
        )
        for e in range(RING)
        for n, (source, held, to) in enumerate(
            ((from_in, in_held, grad_in), (from_out, out_held, grad_out))
        )
    ]
    for pair in gets:
        for get in pair:
            get.start()
    for get, _ in through:
        get.start()
    for get, leave in through:
        get.wait()
        leave.start()
    wide = m_parts.shape[-1]
    for c in range(CHUNKS):
        for get, parts, out in zip(gets[c], (m_held, t_held), (mixed, d_tokens)):
            get.wait()
            total = parts[c, 0].astype(F32)
            for s in range(1, RING):
                total += parts[c, s].astype(F32)
            out[:, pl.ds(c * wide, wide)] = total.astype(BF16)
    for _, leave in through:
        leave.wait()


def body(tokens, d_mixed, w_in, w_out, expert_ids, gate_fixed, placement):
    tok_rows, width = tokens.shape
    hidden = w_out.shape[1]
    wide = width // CHUNKS
    shuttle = pltpu.VMEM((CHUNKS, GROUPS, PEERS, TILE, wide), BF16)
    own = pltpu.VMEM((CHUNKS, RING, tok_rows, wide), BF16)
    dma = pltpu.SemaphoreType.DMA
    anywhere = pl.BlockSpec(memory_space=pl.ANY)
    inside = pl.BlockSpec(memory_space=pltpu.VMEM)
    everyone = RING * tok_rows
    kinds = len(RINGS)
    whole = jax.ShapeDtypeStruct((tok_rows, width), BF16)
    part = jax.ShapeDtypeStruct((CHUNKS, RING, tok_rows, wide), BF16)
    grads = (
        jax.ShapeDtypeStruct((RING, wide, 2 * hidden), BF16),
        jax.ShapeDtypeStruct((RING, hidden, wide), BF16),
    )
    found = pl.pallas_call(
        kernel,
        out_shape=(part, part, *grads),
        in_specs=[anywhere, anywhere, inside, inside, inside, anywhere, anywhere],
        out_specs=[anywhere] * 4,
        scratch_shapes=[
            own, own, shuttle, shuttle, shuttle, shuttle, shuttle, shuttle,
            pltpu.VMEM((kinds, RING, 2, PEERS, tok_rows), F32),
            pltpu.VMEM((kinds, RING, 2, PEERS, tok_rows), F32),
            pltpu.VMEM((width, 2 * hidden), BF16),
            pltpu.VMEM((hidden, width), BF16),
            pltpu.VMEM((kinds, GROUPS, ROWS, everyone), BF16),
            pltpu.VMEM((kinds, GROUPS, ROWS, 1), F32),
            pltpu.VMEM((max(kinds - 1, 1), ROWS, ROWS), BF16),
            pltpu.VMEM((GROUPS, everyone, ROWS), BF16),
            pltpu.VMEM((GROUPS, everyone, ROWS), BF16),
            pltpu.VMEM((GROUPS, ROWS, 2 * hidden), F32),
            pltpu.VMEM((GROUPS, ROWS, hidden), BF16),
            pltpu.VMEM((GROUPS, ROWS, 2 * hidden), BF16),
            pltpu.VMEM((2, wide, 2 * hidden), BF16),
            pltpu.VMEM((2, hidden, wide), BF16),
            dma((2,)), dma((kinds,)), dma((kinds,)), dma((2, CHUNKS)), dma((2, CHUNKS)),
            dma((4, CHUNKS)), dma((4, CHUNKS)), dma((2, CHUNKS)), dma((2, CHUNKS)),
            dma((4,)), dma((4,)), dma((4,)), dma((4,)),
        ],
        compiler_params=pltpu.CompilerParams(
            has_side_effects=True, vmem_limit_bytes=60 * 1024 * 1024
        ),
        cost_estimate=pl.CostEstimate(flops=36 * 10**9, bytes_accessed=30 * 10**6, transcendentals=10**6),
    )(tokens, d_mixed, expert_ids.T, gate_fixed.T, placement.reshape(1, -1), w_in, w_out)
    return pl.pallas_call(
        finish,
        out_shape=(whole, whole, *grads),
        in_specs=[anywhere] * 4,
        out_specs=(inside, inside, anywhere, anywhere),
        scratch_shapes=[
            *[pltpu.VMEM(held.shape, BF16) for held in (part, part, *grads)],
            dma((2, CHUNKS)), dma((2, RING)), dma((2, RING)),
        ],
        compiler_params=pltpu.CompilerParams(vmem_limit_bytes=60 * 1024 * 1024),
    )(*found)


def solution(mesh):
    in_specs = (
        P(ALL, None),
        P(ALL, None),
        P("expert", None, None),
        P("expert", None, None),
        P(ALL, None),
        P(ALL, None),
        P(),
    )
    out_specs = (P(ALL, None), P(ALL, None), P("expert", "dp", None), P("expert", None, "dp"))
    return jax.shard_map(body, mesh=mesh, in_specs=in_specs, out_specs=out_specs, check_vma=False)
```
